512 devices in a mesh: grp: 16 (over x, y), occ: 32 (over z, core).
Axes of the slice: x: 4, y: 4, z: 16, core: 2. Of those that a mesh axis runs over, the one named last changes fastest.
Arguments:
- b_ints: bfloat16 [4096, 768, 256], P(('grp', 'occ')), may hold values from -6 to 6
- osv_vecs: bfloat16 [4096, 768, 128], P(('grp', 'occ')), may hold values from -0.21875 to 0.21875
- inv_denom: float32 [4096, 128], P(('grp', 'occ')), may hold values from 0.5 to 4
- domains: int32 [4096, 6], P('grp'), may hold values from 0 to 95, all different within a row
- dom_count: int32 [4096], P('grp'), may hold values from 1 to 6
- owner_slot: int32 [96], replicated, may hold values from 0 to 95, each once
Outputs:
- gamma_tiles: bfloat16 [256, 96, 128], P('occ', 'grp')
The draws below stay inside these ranges and needn't reach their ends.
Inputs may be any that keep to these rules, and one draw needn't show every extreme that they name: `domains`: each row names distinct tiles.
All inputs are finite; a program needn't handle non-finite values.
Results may differ from the reference program's by a relative error of at most 0.0056.
Values may be sent and summed in bfloat16 or wider, within the bound.
No kernel may reach another device: no remote copies, remote signals or barrier semaphores. Data moves between devices by JAX's collectives and lax.ppermute only.
A program may use at most 64 MiB of HBM per device.

```python
import math
import jax
import jax.numpy as jnp
from jax import lax

TILE = 128
KD = 6
NOSV = 128
NT = 96
NB = 256
NOCC = 4096


def plant(entries, stream_key, low, top_value):
    spot = [jax.random.randint(jax.random.fold_in(stream_key, axis), (), 0, length) for axis, length in enumerate(entries.shape)]
    longest = entries.shape.index(max(entries.shape))
    next_to = spot[:longest] + [(spot[longest] + 1) % entries.shape[longest]] + spot[longest + 1:]
    return entries.at[tuple(spot)].set(low).at[tuple(next_to)].set(top_value)


def levels(key, dims, shards, low, largest):
    gain, own = 1.0, jax.random.fold_in(key, 6)
    for position, blocks in shards:
        steps = jnp.exp(jax.random.uniform(jax.random.fold_in(own, position), (blocks,), jnp.float32, low / len(shards), largest / len(shards)))
        gain = gain * jnp.repeat(steps, dims[position] // blocks).reshape([-1 if axis == position else 1 for axis in range(len(dims))])
    return gain


def picks_of(stream_key, rows, count, top, lift):
    order = jax.random.permutation(jax.random.fold_in(stream_key, 1), count)
    boost = order
    for power in range(3):
        boost = boost * boost // count
    boost = boost * lift // count
    tickets = jax.random.randint(jax.random.fold_in(stream_key, 2), (rows, count), 0, 4096) + boost
    holders = jax.random.permutation(jax.random.fold_in(stream_key, 3), rows)[jnp.arange(count) % rows]
    tickets = jnp.where(jnp.arange(rows)[:, None] == holders[None, :], 1 << 14, tickets)
    priority = tickets * count + jnp.arange(count)
    return lax.top_k(priority.astype(jnp.int32), top)[1].astype(jnp.int32)


def bell_draw(own_key, shape, width, limit, cuts=(), kind=jnp.bfloat16):
    result = width * jax.random.normal(own_key, shape, jnp.float32)
    if cuts:
        result = result * levels(own_key, shape, cuts, -0.22, 0.18)
    return jnp.clip(result, -limit, limit).astype(kind)


def setup_inputs(seed: int = 0) -> dict:
    arg_keys = jax.random.split(jax.random.key(seed), 7)
    b_ints = bell_draw(arg_keys[0], (NOCC, KD * TILE, NB), 1.0, 6.0, ((0, 512),))
    osv_vecs = bell_draw(arg_keys[1], (NOCC, KD * TILE, NOSV), (KD * TILE) ** -0.5, 0.21875, ((0, 512),))
    inv_denom = jnp.clip(jnp.exp(math.log(4.0) - 2.0794415 * jax.random.uniform(arg_keys[2], (NOCC, NOSV), jnp.float32) ** levels(arg_keys[2], (NOCC, NOSV), ((0, 512),), -0.2, 0.2)), 0.5, 4.0)
    domains = picks_of(arg_keys[3], NOCC, NT, KD, 512)
    dom_count = plant(jax.random.randint(arg_keys[4], (NOCC,), 1, KD + 1), jax.random.fold_in(arg_keys[4], 1), 1, KD).astype(jnp.int32)
    owner_slot = jax.random.permutation(arg_keys[5], NT).astype(jnp.int32)
    return dict(b_ints=b_ints, osv_vecs=osv_vecs, inv_denom=inv_denom, domains=domains, dom_count=dom_count, owner_slot=owner_slot)


def reference(b_ints, osv_vecs, inv_denom, domains, dom_count, owner_slot):
    nocc = b_ints.shape[0]
    blocks = nocc // 32
    keep = jnp.arange(KD, dtype=jnp.int32)[None, :] < dom_count[:, None]
    slot = jnp.where(keep, owner_slot[domains], -1).astype(jnp.int32)
    rowmask = jnp.repeat(keep, TILE, axis=1).astype(jnp.float32)
    tiles_ids = jnp.arange(NT, dtype=jnp.int32)

    def step(total, index):
        start = (index * 32).astype(jnp.int32)
        block_b = lax.dynamic_slice_in_dim(b_ints, start, 32, 0).astype(jnp.float32)
        block_q = lax.dynamic_slice_in_dim(osv_vecs, start, 32, 0).astype(jnp.float32)
        block_d = lax.dynamic_slice_in_dim(inv_denom, start, 32, 0)
        block_m = lax.dynamic_slice_in_dim(rowmask, start, 32, 0)
        block_s = lax.dynamic_slice_in_dim(slot, start, 32, 0)
        hidden = jnp.einsum('ikn,ikp->inp', block_q, block_b * block_m[:, :, None])
        scaled = (hidden * block_d[:, :, None]).astype(jnp.bfloat16)
        amp = jnp.einsum('ikn,inp->pik', block_q, scaled.astype(jnp.float32))
        amp = (amp * block_m[None]).astype(jnp.bfloat16)
        inst = amp.reshape(NB, 32 * KD, TILE).astype(jnp.float32)
        onehot = (block_s.reshape(-1)[None, :] == tiles_ids[:, None]).astype(jnp.float32)
        return total + jnp.einsum('sn,pna->psa', onehot, inst), None

    total, _ = lax.scan(step, jnp.zeros((NB, NT, TILE), jnp.float32), jnp.arange(blocks, dtype=jnp.int32))
    return total.astype(jnp.bfloat16)
```

```python
import functools

import jax
import jax.numpy as jnp
from jax import lax
from jax.experimental import pallas as pl
from jax.experimental.pallas import tpu as pltpu
from jax.sharding import PartitionSpec as P

LANES = 8


def amplitudes(kdom, tile, cnt_ref, core_ref, b_ref, q_ref, inv_ref, keep_ref, send_ref):
    i = pl.program_id(0)
    used = cnt_ref[i] * tile
    q = q_ref[0]
    rows = lax.broadcasted_iota(jnp.int32, q.shape, 0)
    q = jnp.where(rows < used, q.astype(jnp.float32), 0.0)
    qt = q.T.astype(jnp.bfloat16)
    h = jnp.dot(qt, b_ref[0], preferred_element_type=jnp.float32)
    ht = h.T * inv_ref[pl.ds(i, 1), :]
    nb, nosv = ht.shape
    ht = ht.reshape(nb // (2 * LANES), 2, LANES, nosv)
    even = ht[:, 0].reshape(nb // 2, nosv)
    odd = ht[:, 1].reshape(nb // 2, nosv)
    first = core_ref[0] == 0
    scaled = jnp.concatenate([jnp.where(first, even, odd), jnp.where(first, odd, even)], 0)
    y = jnp.dot(scaled.astype(jnp.bfloat16), qt, preferred_element_type=jnp.float32)
    y = y.astype(jnp.bfloat16)
    for k in range(kdom):
        keep_ref[k] = y[: nb // 2, k * tile : (k + 1) * tile]
        send_ref[k] = y[nb // 2 :, k * tile : (k + 1) * tile]


def combine(own_slots, got_slots, own_ref, got_ref, out_ref, own_head, own_next, got_head, got_next):
    step = pl.program_id(0)
    block = out_ref.shape[0]
    shape = out_ref.shape[1:]

    @pl.when(step == 0)
    def _():
        for slots, head, link in ((own_slots, own_head, own_next), (got_slots, got_head, got_next)):

            @pl.loop(0, head.shape[0])
            def _(s):
                head[s] = -1

            @pl.loop(0, link.shape[0])
            def _(t):
                s = slots[t]

                @pl.when(s >= 0)
                def _():
                    link[t] = head[s]
                    head[s] = t

    def walk(head, link, ref, slot, total):
        def body(state):
            t, total = state
            return link[t], total + ref[t].astype(jnp.float32)

        return lax.while_loop(lambda state: state[0] >= 0, body, (head[slot], total))[1]

    @pl.loop(0, block)
    def _(j):
        slot = step * block + j
        total = walk(own_head, own_next, own_ref, slot, jnp.zeros(shape, jnp.float32))
        out_ref[j] = walk(got_head, got_next, got_ref, slot, total).astype(out_ref.dtype)


def local(ngrp, nocc, b_ints, osv_vecs, inv_denom, domains, dom_count, owner_slot):
    own, rows, nb = b_ints.shape
    kdom = domains.shape[1]
    tile = rows // kdom
    nosv = osv_vecs.shape[2]
    ntiles = owner_slot.shape[0]
    me = lax.axis_index("occ")
    core = me % 2
    half = nb // 2

    pair = lax.dynamic_slice_in_dim(domains, (me - core) * own, 2 * own, 0)
    counts = lax.dynamic_slice_in_dim(dom_count, (me - core) * own, 2 * own, 0)
    keep = jnp.arange(kdom, dtype=jnp.int32)[None, :] < counts[:, None]
    looked = jnp.sum(jnp.where(pair[:, :, None] == jnp.arange(ntiles, dtype=jnp.int32), owner_slot, 0), axis=-1)
    slots = jnp.where(keep, looked, -1).reshape(2, own * kdom)
    own_slots = lax.dynamic_index_in_dim(slots, core, 0, keepdims=False)
    got_slots = lax.dynamic_index_in_dim(slots, 1 - core, 0, keepdims=False)
    own_counts = lax.dynamic_slice_in_dim(dom_count, me * own, own, 0)

    half_tiles = jax.ShapeDtypeStruct((own * kdom, half, tile), jnp.bfloat16)
    kept, sent = pl.pallas_call(
        functools.partial(amplitudes, kdom, tile),
        grid_spec=pltpu.PrefetchScalarGridSpec(
            num_scalar_prefetch=2,
            grid=(own,),
            in_specs=[
                pl.BlockSpec((1, rows, nb), lambda i, *_: (i, 0, 0)),
                pl.BlockSpec((1, rows, nosv), lambda i, *_: (i, 0, 0)),
                pl.BlockSpec((own, nosv), lambda i, *_: (0, 0)),
            ],
            out_specs=[pl.BlockSpec((kdom, half, tile), lambda i, *_: (i, 0, 0))] * 2,
        ),
        out_shape=[half_tiles, half_tiles],
        compiler_params=pltpu.CompilerParams(vmem_limit_bytes=40 << 20),
        cost_estimate=pl.CostEstimate(flops=4 * own * rows * nb * nosv, bytes_accessed=8 << 20, transcendentals=0),
        name="amplitudes",
    )(own_counts, core.reshape(1), b_ints, osv_vecs, inv_denom)

    got = lax.ppermute(sent, "occ", [(i, i ^ 1) for i in range(nocc)])

    block = 12
    whole = pl.BlockSpec((own * kdom, half, tile), lambda g, *_: (0, 0, 0))
    dense = pl.pallas_call(
        combine,
        grid_spec=pltpu.PrefetchScalarGridSpec(
            num_scalar_prefetch=2,
            grid=(ntiles // block,),
            in_specs=[whole, whole],
            out_specs=pl.BlockSpec((block, half, tile), lambda g, *_: (g, 0, 0)),
            scratch_shapes=[
                pltpu.SMEM((ntiles,), jnp.int32),
                pltpu.SMEM((own * kdom,), jnp.int32),
                pltpu.SMEM((ntiles,), jnp.int32),
                pltpu.SMEM((own * kdom,), jnp.int32),
            ],
        ),
        out_shape=jax.ShapeDtypeStruct((ntiles, half, tile), jnp.bfloat16),
        compiler_params=pltpu.CompilerParams(vmem_limit_bytes=40 << 20),
        cost_estimate=pl.CostEstimate(flops=1 << 22, bytes_accessed=7 << 20, transcendentals=0),
        name="combine",
    )(own_slots, got_slots, kept, got)

    parts = lax.all_to_all(dense, "grp", 0, 0, tiled=True)
    mine = parts.reshape(ngrp, ntiles // ngrp, half, tile).astype(jnp.float32).sum(0).astype(jnp.bfloat16)

    nz = nocc // 2
    columns = [[2 * z + c for z in range(nz)] for c in range(2)]
    blocks = mine.reshape(ntiles // ngrp, nz, LANES, tile).transpose(1, 0, 2, 3)
    parts = lax.all_to_all(blocks, "occ", 0, 0, tiled=True, axis_index_groups=columns)
    return parts.astype(jnp.float32).sum(0).astype(jnp.bfloat16).transpose(1, 0, 2)


def solution(mesh):
    return jax.shard_map(
        functools.partial(local, mesh.shape["grp"], mesh.shape["occ"]),
        mesh=mesh,
        in_specs=(
            P(("grp", "occ"), None, None),
            P(("grp", "occ"), None, None),
            P(("grp", "occ"), None),
            P("grp", None),
            P("grp"),
            P(),
        ),
        out_specs=P("occ", "grp", None),
        check_vma=False,
    )
```

```python
import functools

import jax
import jax.numpy as jnp
from jax import lax
from jax.experimental import pallas as pl
from jax.experimental.pallas import tpu as pltpu
from jax.sharding import PartitionSpec as P

LANES = 8


def amplitudes(kdom, tile, me_ref, cnt_hbm, b_hbm, q_hbm, inv_hbm, keep_hbm, send_hbm, cnt, b_buf, q_buf, inv, keep_ref, send_ref, small, sems):
    own = b_buf.shape[0]
    me = me_ref[0]
    counts = pltpu.make_async_copy(cnt_hbm, cnt, small.at[0])
    counts.start()
    gaps = pltpu.make_async_copy(inv_hbm, inv, small.at[1])
    gaps.start()

    def fetch(i):
        return (
            pltpu.make_async_copy(q_hbm.at[i], q_buf.at[i], sems.at[0, i]),
            pltpu.make_async_copy(b_hbm.at[i], b_buf.at[i], sems.at[1, i]),
        )

    def store(i):
        tiles = pl.ds(i * kdom, kdom)
        return (
            pltpu.make_async_copy(keep_ref.at[tiles], keep_hbm.at[tiles], sems.at[2, i]),
            pltpu.make_async_copy(send_ref.at[tiles], send_hbm.at[tiles], sems.at[3, i]),
        )

    for i in range(own):
        for copy in fetch(i):
            copy.start()
    counts.wait()
    gaps.wait()
    first = me % 2 == 0

    @pl.loop(0, own)
    def _(i):
        for copy in fetch(i):
            copy.wait()
        used = cnt[me * own + i]
        row = inv[pl.ds(i, 1), :]

        def part(tiles):
            rows = tiles * tile
            q = q_buf[i, :rows]
            at = lax.broadcasted_iota(jnp.int32, q.shape, 0)
            masked = jnp.where(at < used * tile, q.astype(jnp.float32), 0.0).astype(jnp.bfloat16)
            h = lax.dot_general(b_buf[i, :rows], masked, (((0,), (0,)), ((), ())), preferred_element_type=jnp.float32)
            h = h * row
            nb, nosv = h.shape
            h = h.reshape(nb // (2 * LANES), 2, LANES, nosv)
            even = h[:, 0].reshape(nb // 2, nosv)
            odd = h[:, 1].reshape(nb // 2, nosv)
            scaled = jnp.concatenate([jnp.where(first, even, odd), jnp.where(first, odd, even)], 0)
            y = lax.dot_general(
                scaled.astype(jnp.bfloat16), q, (((1,), (1,)), ((), ())), preferred_element_type=jnp.float32
            ).astype(jnp.bfloat16)
            for k in range(tiles):
                keep_ref[i * kdom + k] = y[: nb // 2, k * tile : (k + 1) * tile]
                send_ref[i * kdom + k] = y[nb // 2 :, k * tile : (k + 1) * tile]

        for low in range(0, kdom, 2):
            high = min(low + 2, kdom)
            inside = used > low if high == kdom else jnp.logical_and(used > low, used <= high)
            pl.when(inside)(functools.partial(part, high))
        for copy in store(i):
            copy.start()

    @pl.loop(0, own)
    def _(i):
        for copy in store(i):
            copy.wait()


def combine(slot_ref, next_ref, own_ref, got_ref, out_ref):
    half = own_ref.shape[0]
    tiles = 2 * half
    out_ref[...] = jnp.zeros_like(out_ref)

    def tile(t):
        a = own_ref[jnp.minimum(t, half - 1)].astype(jnp.float32)
        b = got_ref[jnp.maximum(t - half, 0)].astype(jnp.float32)
        return jnp.where(t < half, a, b)

    def enter(ref, offset):
        @pl.loop(0, half)
        def _(t):
            slot = slot_ref[t + offset]

            @pl.when(slot >= 0)
            def _():
                after = next_ref[t + offset]

                @pl.when(after >= tiles)
                def _():
                    out_ref[slot] = ref[t]

                @pl.when(after < tiles)
                def _():
                    def body(state):
                        n, total = state
                        return next_ref[n], total + tile(n)

                    total = lax.while_loop(lambda state: state[0] < tiles, body, (after, ref[t].astype(jnp.float32)))[1]
                    out_ref[slot] = total.astype(out_ref.dtype)

    enter(own_ref, 0)
    enter(got_ref, half)


def local(ngrp, nocc, b_ints, osv_vecs, inv_denom, domains, dom_count, owner_slot):
    own, rows, nb = b_ints.shape
    kdom = domains.shape[1]
    tile = rows // kdom
    nosv = osv_vecs.shape[2]
    ntiles = owner_slot.shape[0]
    me = lax.axis_index("occ")
    core = me % 2
    half = nb // 2
    vmem = pl.BlockSpec(memory_space=pltpu.VMEM)
    smem = pl.BlockSpec(memory_space=pltpu.SMEM)
    hbm = pl.BlockSpec(memory_space=pl.ANY)

    half_tiles = jax.ShapeDtypeStruct((own * kdom, half, tile), jnp.bfloat16)
    kept, sent = pl.pallas_call(
        functools.partial(amplitudes, kdom, tile),
        in_specs=[smem, hbm, hbm, hbm, hbm],
        out_specs=[hbm, hbm],
        out_shape=[half_tiles, half_tiles],
        scratch_shapes=[
            pltpu.SMEM(dom_count.shape, jnp.int32),
            pltpu.VMEM(b_ints.shape, b_ints.dtype),
            pltpu.VMEM(osv_vecs.shape, osv_vecs.dtype),
            pltpu.VMEM(inv_denom.shape, inv_denom.dtype),
            pltpu.VMEM(half_tiles.shape, half_tiles.dtype),
            pltpu.VMEM(half_tiles.shape, half_tiles.dtype),
            pltpu.SemaphoreType.DMA((2,)),
            pltpu.SemaphoreType.DMA((4, own)),
        ],
        compiler_params=pltpu.CompilerParams(vmem_limit_bytes=60 << 20),
        cost_estimate=pl.CostEstimate(flops=4 * own * rows * nb * nosv, bytes_accessed=8 << 20, transcendentals=0),
        name="amplitudes",
    )(me.reshape(1), dom_count, b_ints, osv_vecs, inv_denom)

    got = lax.ppermute(sent, "occ", [(i, i ^ 1) for i in range(nocc)])

    base = (me - core) * own
    pair = lax.dynamic_slice_in_dim(domains, base, 2 * own, 0)
    counts = lax.dynamic_slice_in_dim(dom_count, base, 2 * own, 0)
    keep = jnp.arange(kdom, dtype=jnp.int32)[None, :] < counts[:, None]
    looked = jnp.sum(jnp.where(pair[:, :, None] == jnp.arange(ntiles, dtype=jnp.int32), owner_slot, 0), axis=-1)
    slots = jnp.where(keep, looked, -1)
    slots = jnp.where(core == 0, slots, jnp.roll(slots, own, axis=0)).reshape(-1)
    count = slots.shape[0]
    order = jnp.arange(count, dtype=jnp.int32)
    same = slots[:, None] == slots[None, :]
    earlier = jnp.any(same & (order[None, :] < order[:, None]), axis=1)
    heads = jnp.where(earlier, -1, slots)
    after = jnp.min(jnp.where(same & (order[None, :] > order[:, None]), order[None, :], count), axis=1)

    dense = pl.pallas_call(
        combine,
        in_specs=[smem, smem, vmem, vmem],
        out_specs=vmem,
        out_shape=jax.ShapeDtypeStruct((ntiles, half, tile), jnp.bfloat16),
        compiler_params=pltpu.CompilerParams(vmem_limit_bytes=24 << 20),
        cost_estimate=pl.CostEstimate(flops=1 << 22, bytes_accessed=7 << 20, transcendentals=0),
        name="combine",
    )(heads, after, kept, got)

    parts = lax.all_to_all(dense, "grp", 0, 0, tiled=True)
    mine = parts.reshape(ngrp, ntiles // ngrp, half, tile).astype(jnp.float32).sum(0).astype(jnp.bfloat16)

    nz = nocc // 2
    columns = [[2 * z + c for z in range(nz)] for c in range(2)]
    blocks = mine.reshape(ntiles // ngrp, nz, LANES, tile).transpose(1, 0, 2, 3)
    parts = lax.all_to_all(blocks, "occ", 0, 0, tiled=True, axis_index_groups=columns)
    return parts.astype(jnp.float32).sum(0).astype(jnp.bfloat16).transpose(1, 0, 2)


def solution(mesh):
    return jax.shard_map(
        functools.partial(local, mesh.shape["grp"], mesh.shape["occ"]),
        mesh=mesh,
        in_specs=(
            P(("grp", "occ"), None, None),
            P(("grp", "occ"), None, None),
            P(("grp", "occ"), None),
            P("grp", None),
            P("grp"),
            P(),
        ),
        out_specs=P("occ", "grp", None),
        check_vma=False,
    )
```

```python
import functools
import math

import jax
import jax.numpy as jnp
from jax import lax
from jax.experimental import pallas as pl
from jax.experimental.pallas import tpu as pltpu
from jax.sharding import PartitionSpec as P

LANES = 8


def amplitudes(kdom, tile, me_ref, cnt_hbm, b_hbm, q_hbm, inv_hbm, keep_ref, send_hbm, cnt, b_buf, q_buf, inv, send_ref, small, sems):
    own = b_buf.shape[0]
    me = me_ref[0]
    counts = pltpu.make_async_copy(cnt_hbm, cnt, small.at[0])
    counts.start()
    gaps = pltpu.make_async_copy(inv_hbm, inv, small.at[1])
    gaps.start()

    def fetch(i):
        return (
            pltpu.make_async_copy(q_hbm.at[i], q_buf.at[i], sems.at[0, i]),
            pltpu.make_async_copy(b_hbm.at[i], b_buf.at[i], sems.at[1, i]),
        )

    def store(i):
        tiles = pl.ds(i * kdom, kdom)
        return pltpu.make_async_copy(send_ref.at[tiles], send_hbm.at[tiles], sems.at[2, i])

    for i in range(own):
        for copy in fetch(i):
            copy.start()
    counts.wait()
    gaps.wait()
    first = me % 2 == 0

    @pl.loop(0, own)
    def _(i):
        for copy in fetch(i):
            copy.wait()
        used = cnt[me * own + i]
        row = inv[pl.ds(i, 1), :]

        def part(tiles):
            rows = tiles * tile
            q = q_buf[i, :rows]
            at = lax.broadcasted_iota(jnp.int32, q.shape, 0)
            masked = jnp.where(at < used * tile, q.astype(jnp.float32), 0.0).astype(jnp.bfloat16)
            h = lax.dot_general(b_buf[i, :rows], masked, (((0,), (0,)), ((), ())), preferred_element_type=jnp.float32)
            h = h * row
            nb, nosv = h.shape
            h = h.reshape(nb // (2 * LANES), 2, LANES, nosv)
            even = h[:, 0].reshape(nb // 2, nosv)
            odd = h[:, 1].reshape(nb // 2, nosv)
            scaled = jnp.concatenate([jnp.where(first, even, odd), jnp.where(first, odd, even)], 0)
            y = lax.dot_general(
                scaled.astype(jnp.bfloat16), q, (((1,), (1,)), ((), ())), preferred_element_type=jnp.float32
            ).astype(jnp.bfloat16)
            for k in range(tiles):
                keep_ref[i * kdom + k] = y[: nb // 2, k * tile : (k + 1) * tile]
                send_ref[i * kdom + k] = y[nb // 2 :, k * tile : (k + 1) * tile]

        for low in range(0, kdom, 2):
            high = min(low + 2, kdom)
            inside = used > low if high == kdom else jnp.logical_and(used > low, used <= high)
            pl.when(inside)(functools.partial(part, high))
        store(i).start()

    @pl.loop(0, own)
    def _(i):
        store(i).wait()


def combine(slot_ref, next_ref, own_ref, got_ref, out_ref):
    half = own_ref.shape[0]
    tiles = 2 * half
    out_ref[...] = jnp.zeros_like(out_ref)

    def tile(t):
        a = own_ref[jnp.minimum(t, half - 1)].astype(jnp.float32)
        b = got_ref[jnp.maximum(t - half, 0)].astype(jnp.float32)
        return jnp.where(t < half, a, b)

    def enter(ref, offset):
        @pl.loop(0, half)
        def _(t):
            slot = slot_ref[t + offset]

            @pl.when(slot >= 0)
            def _():
                after = next_ref[t + offset]

                @pl.when(after >= tiles)
                def _():
                    out_ref[slot] = ref[t]

                @pl.when(after < tiles)
                def _():
                    def body(state):
                        n, total = state
                        return next_ref[n], total + tile(n)

                    total = lax.while_loop(lambda state: state[0] < tiles, body, (after, ref[t].astype(jnp.float32)))[1]
                    out_ref[slot] = total.astype(out_ref.dtype)

    enter(own_ref, 0)
    enter(got_ref, half)


def local(ngrp, nocc, b_ints, osv_vecs, inv_denom, domains, dom_count, owner_slot):
    own, rows, nb = b_ints.shape
    kdom = domains.shape[1]
    tile = rows // kdom
    nosv = osv_vecs.shape[2]
    ntiles = owner_slot.shape[0]
    me = lax.axis_index("occ")
    core = me % 2
    half = nb // 2
    vmem = pl.BlockSpec(memory_space=pltpu.VMEM)
    smem = pl.BlockSpec(memory_space=pltpu.SMEM)
    hbm = pl.BlockSpec(memory_space=pl.ANY)

    half_tiles = jax.ShapeDtypeStruct((own * kdom, half, tile), jnp.bfloat16)
    kept, sent = pl.pallas_call(
        functools.partial(amplitudes, kdom, tile),
        in_specs=[smem, hbm, hbm, hbm, hbm],
        out_specs=[vmem, hbm],
        out_shape=[half_tiles, half_tiles],
        scratch_shapes=[
            pltpu.SMEM(dom_count.shape, jnp.int32),
            pltpu.VMEM(b_ints.shape, b_ints.dtype),
            pltpu.VMEM(osv_vecs.shape, osv_vecs.dtype),
            pltpu.VMEM(inv_denom.shape, inv_denom.dtype),
            pltpu.VMEM(half_tiles.shape, half_tiles.dtype),
            pltpu.SemaphoreType.DMA((2,)),
            pltpu.SemaphoreType.DMA((3, own)),
        ],
        compiler_params=pltpu.CompilerParams(vmem_limit_bytes=52 << 20),
        cost_estimate=pl.CostEstimate(flops=4 * own * rows * nb * nosv, bytes_accessed=8 << 20, transcendentals=0),
        name="amplitudes",
    )(me.reshape(1), dom_count, b_ints, osv_vecs, inv_denom)

    got = lax.ppermute(sent, "occ", [(i, i ^ 1) for i in range(nocc)])

    base = (me - core) * own
    pair = lax.dynamic_slice_in_dim(domains, base, 2 * own, 0)
    counts = lax.dynamic_slice_in_dim(dom_count, base, 2 * own, 0)
    keep = jnp.arange(kdom, dtype=jnp.int32)[None, :] < counts[:, None]
    side = math.isqrt(ngrp)
    each = ntiles // ngrp
    owner, within = owner_slot // each, owner_slot % each
    turned = ((owner % side) * side + owner // side) * each + within
    places = jnp.where(core == 0, owner_slot, turned)
    looked = jnp.sum(jnp.where(pair[:, :, None] == jnp.arange(ntiles, dtype=jnp.int32), places, 0), axis=-1)
    slots = jnp.where(keep, looked, -1)
    slots = jnp.where(core == 0, slots, jnp.roll(slots, own, axis=0)).reshape(-1)
    count = slots.shape[0]
    order = jnp.arange(count, dtype=jnp.int32)
    same = slots[:, None] == slots[None, :]
    earlier = jnp.any(same & (order[None, :] < order[:, None]), axis=1)
    heads = jnp.where(earlier, -1, slots)
    after = jnp.min(jnp.where(same & (order[None, :] > order[:, None]), order[None, :], count), axis=1)

    dense = pl.pallas_call(
        combine,
        in_specs=[smem, smem, vmem, vmem],
        out_specs=vmem,
        out_shape=jax.ShapeDtypeStruct((ntiles, half, tile), jnp.bfloat16),
        compiler_params=pltpu.CompilerParams(vmem_limit_bytes=24 << 20),
        cost_estimate=pl.CostEstimate(flops=1 << 22, bytes_accessed=7 << 20, transcendentals=0),
        name="combine",
    )(heads, after, kept, got)

    def line(along, fixed, z, c):
        chips = [(t, fixed) if along == 0 else (fixed, t) for t in range(side)]
        return [(x * side + y) * nocc + 2 * z + c for x, y in chips]

    def stage(tiles, number):
        groups = [line(number ^ c, fixed, z, c) for c in range(2) for z in range(nocc // 2) for fixed in range(side)]
        parts = lax.all_to_all(tiles, ("grp", "occ"), 0, 0, tiled=True, axis_index_groups=groups)
        parts = parts.reshape(side, tiles.shape[0] // side, half, tile)
        return parts.astype(jnp.float32).sum(0).astype(jnp.bfloat16)

    mine = stage(stage(dense, 0), 1)

    nz = nocc // 2
    columns = [[2 * z + c for z in range(nz)] for c in range(2)]
    blocks = mine.reshape(ntiles // ngrp, nz, LANES, tile).transpose(1, 0, 2, 3)
    parts = lax.all_to_all(blocks, "occ", 0, 0, tiled=True, axis_index_groups=columns)
    return parts.astype(jnp.float32).sum(0).astype(jnp.bfloat16).transpose(1, 0, 2)


def solution(mesh):
    return jax.shard_map(
        functools.partial(local, mesh.shape["grp"], mesh.shape["occ"]),
        mesh=mesh,
        in_specs=(
            P(("grp", "occ"), None, None),
            P(("grp", "occ"), None, None),
            P(("grp", "occ"), None),
            P("grp", None),
            P("grp"),
            P(),
        ),
        out_specs=P("occ", "grp", None),
        check_vma=False,
    )
```

```python
import functools
import math

import jax
import jax.numpy as jnp
from jax import lax
from jax.experimental import pallas as pl
from jax.experimental.pallas import tpu as pltpu
from jax.sharding import PartitionSpec as P

LANES = 8


def amplitudes(kdom, tile, me_ref, cnt_hbm, b_hbm, q_hbm, inv_hbm, keep_ref, send_hbm, cnt, b_buf, q_buf, inv, send_ref, small, sems):
    own = b_buf.shape[0]
    me = me_ref[0]
    counts = pltpu.make_async_copy(cnt_hbm, cnt, small.at[0])
    counts.start()
    gaps = pltpu.make_async_copy(inv_hbm, inv, small.at[1])
    gaps.start()

    def fetch(i):
        return (
            pltpu.make_async_copy(q_hbm.at[i], q_buf.at[i], sems.at[0, i]),
            pltpu.make_async_copy(b_hbm.at[i], b_buf.at[i], sems.at[1, i]),
        )

    def store(i):
        tiles = pl.ds(i * kdom, kdom)
        return pltpu.make_async_copy(send_ref.at[tiles], send_hbm.at[tiles], sems.at[2, i])

    for i in range(own):
        for copy in fetch(i):
            copy.start()
    counts.wait()
    gaps.wait()
    first = me % 2 == 0

    @pl.loop(0, own)
    def _(i):
        for copy in fetch(i):
            copy.wait()
        used = cnt[me * own + i]
        row = inv[pl.ds(i, 1), :]

        def part(tiles):
            rows = tiles * tile
            q = q_buf[i, :rows]
            h = lax.dot_general(b_buf[i, :rows], q, (((0,), (0,)), ((), ())), preferred_element_type=jnp.float32)
            h = h * row
            nb, nosv = h.shape
            h = h.reshape(nb // (4 * LANES), 4, LANES, nosv)
            even = jnp.concatenate([h[:, z].reshape(nb // 4, nosv) for z in (0, 2)], 0)
            odd = jnp.concatenate([h[:, z].reshape(nb // 4, nosv) for z in (1, 3)], 0)
            scaled = jnp.concatenate([jnp.where(first, even, odd), jnp.where(first, odd, even)], 0)
            y = lax.dot_general(
                scaled.astype(jnp.bfloat16), q, (((1,), (1,)), ((), ())), preferred_element_type=jnp.float32
            ).astype(jnp.bfloat16)
            for k in range(tiles):
                keep_ref[i * kdom + k] = y[: nb // 2, k * tile : (k + 1) * tile]
                send_ref[i * kdom + k] = y[nb // 2 :, k * tile : (k + 1) * tile]

        for tiles in range(1, kdom + 1):
            pl.when(used == tiles)(functools.partial(part, tiles))
        store(i).start()

    @pl.loop(0, own)
    def _(i):
        store(i).wait()


def place(each, heads, after, tiles_ref, out_ref, base):
    count = tiles_ref.shape[0]
    rows = out_ref.shape[1]

    @pl.loop(0, count)
    def _(t):
        slot = heads[t]

        @pl.when(slot >= 0)
        def _():
            at = slot // each * (2 * each) + slot % each
            following = after[t]

            def put(total):
                out_ref[at] = total[:rows]
                out_ref[at + each] = total[rows:]

            def summed(total):
                def body(state):
                    n, total = state
                    return after[n], total + tiles_ref[n].astype(jnp.float32)

                total = total + tiles_ref[t].astype(jnp.float32)
                put(lax.while_loop(lambda state: state[0] < count, body, (following, total))[1].astype(out_ref.dtype))

            if base is None:
                pl.when(following >= count)(lambda: put(tiles_ref[t]))
                pl.when(following < count)(lambda: summed(0.0))
            else:
                summed(jnp.concatenate([base[at], base[at + each]], 0).astype(jnp.float32))


def place_own(each, heads, after, own_ref, out_ref):
    out_ref[...] = jnp.zeros_like(out_ref)
    place(each, heads, after, own_ref, out_ref, None)


def place_got(each, heads, after, got_ref, base_ref, out_ref):
    place(each, heads, after, got_ref, out_ref, out_ref)


def add_parts(parts_ref, out_ref):
    @pl.loop(0, out_ref.shape[0])
    def _(t):
        total = parts_ref[0, t].astype(jnp.float32)
        for part in range(1, parts_ref.shape[0]):
            total = total + parts_ref[part, t].astype(jnp.float32)
        out_ref[t] = total.astype(out_ref.dtype)


def local(ngrp, nocc, b_ints, osv_vecs, inv_denom, domains, dom_count, owner_slot):
    own, rows, nb = b_ints.shape
    kdom = domains.shape[1]
    tile = rows // kdom
    nosv = osv_vecs.shape[2]
    ntiles = owner_slot.shape[0]
    me = lax.axis_index("occ")
    core = me % 2
    half = nb // 2
    vmem = pl.BlockSpec(memory_space=pltpu.VMEM)
    smem = pl.BlockSpec(memory_space=pltpu.SMEM)
    hbm = pl.BlockSpec(memory_space=pl.ANY)

    half_tiles = jax.ShapeDtypeStruct((own * kdom, half, tile), jnp.bfloat16)
    kept, sent = pl.pallas_call(
        functools.partial(amplitudes, kdom, tile),
        in_specs=[smem, hbm, hbm, hbm, hbm],
        out_specs=[vmem, hbm],
        out_shape=[half_tiles, half_tiles],
        scratch_shapes=[
            pltpu.SMEM(dom_count.shape, jnp.int32),
            pltpu.VMEM(b_ints.shape, b_ints.dtype),
            pltpu.VMEM(osv_vecs.shape, osv_vecs.dtype),
            pltpu.VMEM(inv_denom.shape, inv_denom.dtype),
            pltpu.VMEM(half_tiles.shape, half_tiles.dtype),
            pltpu.SemaphoreType.DMA((2,)),
            pltpu.SemaphoreType.DMA((3, own)),
        ],
        compiler_params=pltpu.CompilerParams(vmem_limit_bytes=52 << 20),
        cost_estimate=pl.CostEstimate(flops=4 * own * rows * nb * nosv, bytes_accessed=8 << 20, transcendentals=0),
        name="amplitudes",
    )(me.reshape(1), dom_count, b_ints, osv_vecs, inv_denom)

    got = lax.ppermute(sent, "occ", [(i, i ^ 1) for i in range(nocc)])

    base = (me - core) * own
    pair = lax.dynamic_slice_in_dim(domains, base, 2 * own, 0)
    counts = lax.dynamic_slice_in_dim(dom_count, base, 2 * own, 0)
    keep = jnp.arange(kdom, dtype=jnp.int32)[None, :] < counts[:, None]
    side = math.isqrt(ngrp)
    each = ntiles // ngrp
    owner, within = owner_slot // each, owner_slot % each
    turned = ((owner % side) * side + owner // side) * each + within
    places = jnp.where(core == 0, owner_slot, turned)
    looked = jnp.sum(jnp.where(pair[:, :, None] == jnp.arange(ntiles, dtype=jnp.int32), places, 0), axis=-1)
    slots = jnp.where(keep, looked, -1)
    slots = jnp.where(core == 0, slots, jnp.roll(slots, own, axis=0)).reshape(2, own * kdom)
    order = jnp.arange(own * kdom, dtype=jnp.int32)
    same = slots[:, :, None] == slots[:, None, :]
    earlier = jnp.any(same & (order[None, :] < order[:, None]), axis=2)
    heads = jnp.where(earlier, -1, slots)
    after = jnp.min(jnp.where(same & (order[None, :] > order[:, None]), order[None, :], own * kdom), axis=2)

    grid = jax.ShapeDtypeStruct((2 * ntiles, half // 2, tile), jnp.bfloat16)
    dense = pl.pallas_call(
        functools.partial(place_own, each),
        in_specs=[smem, smem, vmem],
        out_specs=vmem,
        out_shape=grid,
        compiler_params=pltpu.CompilerParams(vmem_limit_bytes=24 << 20),
        cost_estimate=pl.CostEstimate(flops=1 << 21, bytes_accessed=2 << 20, transcendentals=0),
        name="place_own",
    )(heads[0], after[0], kept)
    dense = pl.pallas_call(
        functools.partial(place_got, each),
        in_specs=[smem, smem, vmem, vmem],
        out_specs=vmem,
        out_shape=grid,
        input_output_aliases={3: 0},
        compiler_params=pltpu.CompilerParams(vmem_limit_bytes=24 << 20),
        name="place_got",
    )(heads[1], after[1], got, dense)

    nz = nocc // 2

    def line(along, fixed, z, c):
        chips = [(t, fixed) if along == 0 else (fixed, t) for t in range(side)]
        return [(x * side + y) * nocc + 2 * z + c for x, y in chips]

    def summed(tiles, axes, groups):
        parts = lax.all_to_all(tiles, axes, 0, 0, tiled=True, axis_index_groups=groups)
        members = len(groups[0])
        parts = parts.reshape(members, tiles.shape[0] // members, *tiles.shape[1:])
        if parts.size < dense.size:
            return parts.astype(jnp.float32).sum(0).astype(jnp.bfloat16)
        return pl.pallas_call(
            add_parts,
            in_specs=[vmem],
            out_specs=vmem,
            out_shape=jax.ShapeDtypeStruct(parts.shape[1:], parts.dtype),
            compiler_params=pltpu.CompilerParams(vmem_limit_bytes=24 << 20),
            name="add_parts",
        )(parts)

    both = ("grp", "occ")
    lines = [line(c, fixed, z, c) for c in range(2) for z in range(nz) for fixed in range(side)]
    mine = summed(dense, both, lines)
    planes = []
    for c in range(2):
        for z in range(0, nz, 2):
            for fixed in range(side):
                even = line(1 - c, fixed, z, c)
                odd = line(1 - c, fixed, (z + 1 - 2 * c) % nz, c)
                planes.append([device for pair in zip(even, odd) for device in pair])
    mine = summed(mine, both, planes)
    columns = [[2 * z + c for z in range(e, nz, 2)] for e in range(2) for c in range(2)]
    blocks = mine.reshape(each, nz // 2, LANES, tile).transpose(1, 0, 2, 3)
    blocks = blocks.reshape(nz // 2 * each, LANES, tile)
    return summed(blocks, "occ", columns).transpose(1, 0, 2)


def solution(mesh):
    return jax.shard_map(
        functools.partial(local, mesh.shape["grp"], mesh.shape["occ"]),
        mesh=mesh,
        in_specs=(
            P(("grp", "occ"), None, None),
            P(("grp", "occ"), None, None),
            P(("grp", "occ"), None),
            P("grp", None),
            P("grp"),
            P(),
        ),
        out_specs=P("occ", "grp", None),
        check_vma=False,
    )
```

```python
import functools
import math

import jax
import jax.numpy as jnp
from jax import lax
from jax.experimental import pallas as pl
from jax.experimental.pallas import tpu as pltpu
from jax.sharding import PartitionSpec as P

LANES = 8
START = 5


def amplitudes(kdom, tile, me_ref, cnt_hbm, b_hbm, q_hbm, inv_hbm, keep_ref, send_hbm, cnt, b_buf, q_buf, inv, send_ref, small, sems):
    own = b_buf.shape[0]
    me = me_ref[0]
    counts = pltpu.make_async_copy(cnt_hbm, cnt, small.at[0])
    counts.start()
    gaps = pltpu.make_async_copy(inv_hbm, inv, small.at[1])
    gaps.start()

    def fetch(i):
        return (
            pltpu.make_async_copy(q_hbm.at[i], q_buf.at[i], sems.at[0, i]),
            pltpu.make_async_copy(b_hbm.at[i], b_buf.at[i], sems.at[1, i]),
        )

    def store(i):
        tiles = pl.ds(i * kdom, kdom)
        return pltpu.make_async_copy(send_ref.at[tiles], send_hbm.at[tiles], sems.at[2, i])

    for i in range(own):
        for copy in fetch(i):
            copy.start()
    counts.wait()
    gaps.wait()
    first = me % 2 == 0

    @pl.loop(0, own)
    def _(i):
        for copy in fetch(i):
            copy.wait()
        used = cnt[me * own + i]
        row = inv[pl.ds(i, 1), :]

        def part(tiles):
            rows = tiles * tile
            q = q_buf[i, :rows]
            h = lax.dot_general(b_buf[i, :rows], q, (((0,), (0,)), ((), ())), preferred_element_type=jnp.float32)
            h = h * row
            nb, nosv = h.shape
            h = h.reshape(nb // (4 * LANES), 4, LANES, nosv)
            h = jnp.concatenate([h[START:], h[:START]], 0)
            even = jnp.concatenate([h[:, z].reshape(nb // 4, nosv) for z in (0, 2)], 0)
            odd = jnp.concatenate([h[:, z].reshape(nb // 4, nosv) for z in (1, 3)], 0)
            scaled = jnp.concatenate([jnp.where(first, even, odd), jnp.where(first, odd, even)], 0)
            y = lax.dot_general(
                scaled.astype(jnp.bfloat16), q, (((1,), (1,)), ((), ())), preferred_element_type=jnp.float32
            ).astype(jnp.bfloat16)
            for k in range(tiles):
                keep_ref[i * kdom + k] = y[: nb // 2, k * tile : (k + 1) * tile]
                send_ref[i * kdom + k] = y[nb // 2 :, k * tile : (k + 1) * tile]

        for tiles in range(1, kdom + 1):
            pl.when(used == tiles)(functools.partial(part, tiles))
        store(i).start()

    @pl.loop(0, own)
    def _(i):
        store(i).wait()


def place(each, heads, after, tiles_ref, out_ref, base):
    count = tiles_ref.shape[0]
    rows = out_ref.shape[1]

    @pl.loop(0, count)
    def _(t):
        slot = heads[t]

        @pl.when(slot >= 0)
        def _():
            at = slot // each * (2 * each) + slot % each
            following = after[t]

            def put(total):
                out_ref[at] = total[:rows]
                out_ref[at + each] = total[rows:]

            def summed(total):
                def body(state):
                    n, total = state
                    return after[n], total + tiles_ref[n].astype(jnp.float32)

                total = total + tiles_ref[t].astype(jnp.float32)
                put(lax.while_loop(lambda state: state[0] < count, body, (following, total))[1].astype(out_ref.dtype))

            if base is None:
                pl.when(following >= count)(lambda: put(tiles_ref[t]))
                pl.when(following < count)(lambda: summed(0.0))
            else:
                summed(jnp.concatenate([base[at], base[at + each]], 0).astype(jnp.float32))


def place_own(each, heads, after, own_ref, out_ref):
    out_ref[...] = jnp.zeros_like(out_ref)
    place(each, heads, after, own_ref, out_ref, None)


def place_got(each, heads, after, got_ref, base_ref, out_ref):
    place(each, heads, after, got_ref, out_ref, out_ref)


def add_parts(parts_ref, out_ref):
    @pl.loop(0, out_ref.shape[0])
    def _(t):
        total = parts_ref[0, t].astype(jnp.float32)
        for part in range(1, parts_ref.shape[0]):
            total = total + parts_ref[part, t].astype(jnp.float32)
        out_ref[t] = total.astype(out_ref.dtype)


def local(ngrp, nocc, b_ints, osv_vecs, inv_denom, domains, dom_count, owner_slot):
    own, rows, nb = b_ints.shape
    kdom = domains.shape[1]
    tile = rows // kdom
    nosv = osv_vecs.shape[2]
    ntiles = owner_slot.shape[0]
    me = lax.axis_index("occ")
    core = me % 2
    half = nb // 2
    vmem = pl.BlockSpec(memory_space=pltpu.VMEM)
    smem = pl.BlockSpec(memory_space=pltpu.SMEM)
    hbm = pl.BlockSpec(memory_space=pl.ANY)

    half_tiles = jax.ShapeDtypeStruct((own * kdom, half, tile), jnp.bfloat16)
    kept, sent = pl.pallas_call(
        functools.partial(amplitudes, kdom, tile),
        in_specs=[smem, hbm, hbm, hbm, hbm],
        out_specs=[vmem, hbm],
        out_shape=[half_tiles, half_tiles],
        scratch_shapes=[
            pltpu.SMEM(dom_count.shape, jnp.int32),
            pltpu.VMEM(b_ints.shape, b_ints.dtype),
            pltpu.VMEM(osv_vecs.shape, osv_vecs.dtype),
            pltpu.VMEM(inv_denom.shape, inv_denom.dtype),
            pltpu.VMEM(half_tiles.shape, half_tiles.dtype),
            pltpu.SemaphoreType.DMA((2,)),
            pltpu.SemaphoreType.DMA((3, own)),
        ],
        compiler_params=pltpu.CompilerParams(vmem_limit_bytes=52 << 20),
        cost_estimate=pl.CostEstimate(flops=4 * own * rows * nb * nosv, bytes_accessed=8 << 20, transcendentals=0),
        name="amplitudes",
    )(me.reshape(1), dom_count, b_ints, osv_vecs, inv_denom)

    got = lax.ppermute(sent, "occ", [(i, i ^ 1) for i in range(nocc)])

    base = (me - core) * own
    pair = lax.dynamic_slice_in_dim(domains, base, 2 * own, 0)
    counts = lax.dynamic_slice_in_dim(dom_count, base, 2 * own, 0)
    keep = jnp.arange(kdom, dtype=jnp.int32)[None, :] < counts[:, None]
    side = math.isqrt(ngrp)
    each = ntiles // ngrp
    owner, within = owner_slot // each, owner_slot % each
    turned = ((owner % side) * side + owner // side) * each + within
    places = jnp.where(core == 0, owner_slot, turned)
    looked = jnp.sum(jnp.where(pair[:, :, None] == jnp.arange(ntiles, dtype=jnp.int32), places, 0), axis=-1)
    slots = jnp.where(keep, looked, -1)
    slots = jnp.where(core == 0, slots, jnp.roll(slots, own, axis=0)).reshape(2, own * kdom)
    order = jnp.arange(own * kdom, dtype=jnp.int32)
    same = slots[:, :, None] == slots[:, None, :]
    earlier = jnp.any(same & (order[None, :] < order[:, None]), axis=2)
    heads = jnp.where(earlier, -1, slots)
    after = jnp.min(jnp.where(same & (order[None, :] > order[:, None]), order[None, :], own * kdom), axis=2)

    grid = jax.ShapeDtypeStruct((2 * ntiles, half // 2, tile), jnp.bfloat16)
    dense = pl.pallas_call(
        functools.partial(place_own, side * each),
        in_specs=[smem, smem, vmem],
        out_specs=vmem,
        out_shape=grid,
        compiler_params=pltpu.CompilerParams(vmem_limit_bytes=24 << 20),
        cost_estimate=pl.CostEstimate(flops=1 << 21, bytes_accessed=2 << 20, transcendentals=0),
        name="place_own",
    )(heads[0], after[0], kept)
    dense = pl.pallas_call(
        functools.partial(place_got, side * each),
        in_specs=[smem, smem, vmem, vmem],
        out_specs=vmem,
        out_shape=grid,
        input_output_aliases={3: 0},
        compiler_params=pltpu.CompilerParams(vmem_limit_bytes=24 << 20),
        name="place_got",
    )(heads[1], after[1], got, dense)

    nz = nocc // 2

    def line(along, fixed, z, c):
        chips = [(t, fixed) if along == 0 else (fixed, t) for t in range(side)]
        return [(x * side + y) * nocc + 2 * z + c for x, y in chips]

    def summed(tiles, axes, groups):
        parts = lax.all_to_all(tiles, axes, 0, 0, tiled=True, axis_index_groups=groups)
        members = len(groups[0])
        parts = parts.reshape(members, tiles.shape[0] // members, *tiles.shape[1:])
        if parts.size < dense.size:
            return parts.astype(jnp.float32).sum(0).astype(jnp.bfloat16)
        return pl.pallas_call(
            add_parts,
            in_specs=[vmem],
            out_specs=vmem,
            out_shape=jax.ShapeDtypeStruct(parts.shape[1:], parts.dtype),
            compiler_params=pltpu.CompilerParams(vmem_limit_bytes=24 << 20),
            name="add_parts",
        )(parts)

    both = ("grp", "occ")
    lines = [line(c, fixed, z, c) for c in range(2) for z in range(nz) for fixed in range(side)]
    mine = summed(dense, both, lines)
    planes = []
    for c in range(2):
        for z in range(0, nz, 2):
            for fixed in range(side):
                even = line(1 - c, fixed, z, c)
                odd = line(1 - c, fixed, (z + 1 - 2 * c) % nz, c)
                planes.append(even + odd)
    mine = summed(mine, both, planes)
    order = [(z + START) % (nz // 2) for z in range(nz // 2)]
    columns = [[2 * (2 * z + e) + c for z in order] for e in range(2) for c in range(2)]
    blocks = mine.reshape(each, nz // 2, LANES, tile).transpose(1, 0, 2, 3)
    blocks = blocks.reshape(nz // 2 * each, LANES, tile)
    return summed(blocks, "occ", columns).transpose(1, 0, 2)


def solution(mesh):
    return jax.shard_map(
        functools.partial(local, mesh.shape["grp"], mesh.shape["occ"]),
        mesh=mesh,
        in_specs=(
            P(("grp", "occ"), None, None),
            P(("grp", "occ"), None, None),
            P(("grp", "occ"), None),
            P("grp", None),
            P("grp"),
            P(),
        ),
        out_specs=P("occ", "grp", None),
        check_vma=False,
    )
```

```python
import functools
import math

import jax
import jax.numpy as jnp
from jax import lax
from jax.experimental import pallas as pl
from jax.experimental.pallas import tpu as pltpu
from jax.sharding import PartitionSpec as P

LANES = 8
TURN = 2
START = 5


def amplitudes(kdom, tile, me_ref, cnt_hbm, b_hbm, q_hbm, inv_hbm, keep_ref, send_hbm, cnt, b_buf, q_buf, inv, send_ref, small, sems):
    own = b_buf.shape[0]
    me = me_ref[0]
    counts = pltpu.make_async_copy(cnt_hbm, cnt, small.at[0])
    counts.start()
    gaps = pltpu.make_async_copy(inv_hbm, inv, small.at[1])
    gaps.start()

    def fetch(i):
        return (
            pltpu.make_async_copy(q_hbm.at[i], q_buf.at[i], sems.at[0, i]),
            pltpu.make_async_copy(b_hbm.at[i], b_buf.at[i], sems.at[1, i]),
        )

    def store(i):
        tiles = pl.ds(i * kdom, kdom)
        return pltpu.make_async_copy(send_ref.at[tiles], send_hbm.at[tiles], sems.at[2, i])

    for i in range(own):
        for copy in fetch(i):
            copy.start()
    counts.wait()
    gaps.wait()
    first = me % 2 == 0

    @pl.loop(0, own)
    def _(i):
        for copy in fetch(i):
            copy.wait()
        used = cnt[me * own + i]
        row = inv[pl.ds(i, 1), :]

        def part(tiles):
            rows = tiles * tile
            q = q_buf[i, :rows]
            h = lax.dot_general(b_buf[i, :rows], q, (((0,), (0,)), ((), ())), preferred_element_type=jnp.float32)
            h = h * row
            nb, nosv = h.shape
            h = h.reshape(nb // (4 * LANES), 4, LANES, nosv)
            h = jnp.concatenate([h[START:], h[:START]], 0)
            even = jnp.concatenate([h[:, z].reshape(nb // 4, nosv) for z in (0, 2)], 0)
            odd = jnp.concatenate([h[:, z].reshape(nb // 4, nosv) for z in (1, 3)], 0)
            scaled = jnp.concatenate([jnp.where(first, even, odd), jnp.where(first, odd, even)], 0)
            y = lax.dot_general(
                scaled.astype(jnp.bfloat16), q, (((1,), (1,)), ((), ())), preferred_element_type=jnp.float32
            ).astype(jnp.bfloat16)
            for k in range(tiles):
                keep_ref[i * kdom + k] = y[: nb // 2, k * tile : (k + 1) * tile]
                send_ref[i * kdom + k] = y[nb // 2 :, k * tile : (k + 1) * tile]

        for tiles in range(1, kdom + 1):
            pl.when(used == tiles)(functools.partial(part, tiles))
        store(i).start()

    @pl.loop(0, own)
    def _(i):
        store(i).wait()


def place(each, heads, after, tiles_ref, out_ref, base):
    count = tiles_ref.shape[0]
    rows = out_ref.shape[1]

    @pl.loop(0, count)
    def _(t):
        slot = heads[t]

        @pl.when(slot >= 0)
        def _():
            at = slot // each * (2 * each) + slot % each
            following = after[t]

            def put(total):
                out_ref[at] = total[:rows]
                out_ref[at + each] = total[rows:]

            def summed(total):
                def body(state):
                    n, total = state
                    return after[n], total + tiles_ref[n].astype(jnp.float32)

                total = total + tiles_ref[t].astype(jnp.float32)
                put(lax.while_loop(lambda state: state[0] < count, body, (following, total))[1].astype(out_ref.dtype))

            if base is None:
                pl.when(following >= count)(lambda: put(tiles_ref[t]))
                pl.when(following < count)(lambda: summed(0.0))
            else:
                summed(jnp.concatenate([base[at], base[at + each]], 0).astype(jnp.float32))


def place_own(each, heads, after, own_ref, out_ref):
    out_ref[...] = jnp.zeros_like(out_ref)
    place(each, heads, after, own_ref, out_ref, None)


def place_got(each, heads, after, got_ref, base_ref, out_ref):
    place(each, heads, after, got_ref, out_ref, out_ref)


def add_parts(parts_ref, out_ref):
    @pl.loop(0, out_ref.shape[0])
    def _(t):
        total = parts_ref[0, t].astype(jnp.float32)
        for part in range(1, parts_ref.shape[0]):
            total = total + parts_ref[part, t].astype(jnp.float32)
        out_ref[t] = total.astype(out_ref.dtype)


def local(ngrp, nocc, b_ints, osv_vecs, inv_denom, domains, dom_count, owner_slot):
    own, rows, nb = b_ints.shape
    kdom = domains.shape[1]
    tile = rows // kdom
    nosv = osv_vecs.shape[2]
    ntiles = owner_slot.shape[0]
    me = lax.axis_index("occ")
    core = me % 2
    half = nb // 2
    vmem = pl.BlockSpec(memory_space=pltpu.VMEM)
    smem = pl.BlockSpec(memory_space=pltpu.SMEM)
    hbm = pl.BlockSpec(memory_space=pl.ANY)

    half_tiles = jax.ShapeDtypeStruct((own * kdom, half, tile), jnp.bfloat16)
    kept, sent = pl.pallas_call(
        functools.partial(amplitudes, kdom, tile),
        in_specs=[smem, hbm, hbm, hbm, hbm],
        out_specs=[vmem, hbm],
        out_shape=[half_tiles, half_tiles],
        scratch_shapes=[
            pltpu.SMEM(dom_count.shape, jnp.int32),
            pltpu.VMEM(b_ints.shape, b_ints.dtype),
            pltpu.VMEM(osv_vecs.shape, osv_vecs.dtype),
            pltpu.VMEM(inv_denom.shape, inv_denom.dtype),
            pltpu.VMEM(half_tiles.shape, half_tiles.dtype),
            pltpu.SemaphoreType.DMA((2,)),
            pltpu.SemaphoreType.DMA((3, own)),
        ],
        compiler_params=pltpu.CompilerParams(vmem_limit_bytes=52 << 20),
        cost_estimate=pl.CostEstimate(flops=4 * own * rows * nb * nosv, bytes_accessed=8 << 20, transcendentals=0),
        name="amplitudes",
    )(me.reshape(1), dom_count, b_ints, osv_vecs, inv_denom)

    got = lax.ppermute(sent, "occ", [(i, i ^ 1) for i in range(nocc)])

    base = (me - core) * own
    pair = lax.dynamic_slice_in_dim(domains, base, 2 * own, 0)
    counts = lax.dynamic_slice_in_dim(dom_count, base, 2 * own, 0)
    keep = jnp.arange(kdom, dtype=jnp.int32)[None, :] < counts[:, None]
    side = math.isqrt(ngrp)
    each = ntiles // ngrp
    owner, within = owner_slot // each, owner_slot % each
    along_x, along_y = (owner // side - TURN) % side, (owner % side - TURN) % side
    first, second = jnp.where(core == 0, along_x, along_y), jnp.where(core == 0, along_y, along_x)
    places = (first * side + second) * each + within
    looked = jnp.sum(jnp.where(pair[:, :, None] == jnp.arange(ntiles, dtype=jnp.int32), places, 0), axis=-1)
    slots = jnp.where(keep, looked, -1)
    slots = jnp.where(core == 0, slots, jnp.roll(slots, own, axis=0)).reshape(2, own * kdom)
    order = jnp.arange(own * kdom, dtype=jnp.int32)
    same = slots[:, :, None] == slots[:, None, :]
    earlier = jnp.any(same & (order[None, :] < order[:, None]), axis=2)
    heads = jnp.where(earlier, -1, slots)
    after = jnp.min(jnp.where(same & (order[None, :] > order[:, None]), order[None, :], own * kdom), axis=2)

    grid = jax.ShapeDtypeStruct((2 * ntiles, half // 2, tile), jnp.bfloat16)
    dense = pl.pallas_call(
        functools.partial(place_own, side * each),
        in_specs=[smem, smem, vmem],
        out_specs=vmem,
        out_shape=grid,
        compiler_params=pltpu.CompilerParams(vmem_limit_bytes=24 << 20),
        cost_estimate=pl.CostEstimate(flops=1 << 21, bytes_accessed=2 << 20, transcendentals=0),
        name="place_own",
    )(heads[0], after[0], kept)
    dense = pl.pallas_call(
        functools.partial(place_got, side * each),
        in_specs=[smem, smem, vmem, vmem],
        out_specs=vmem,
        out_shape=grid,
        input_output_aliases={3: 0},
        compiler_params=pltpu.CompilerParams(vmem_limit_bytes=24 << 20),
        name="place_got",
    )(heads[1], after[1], got, dense)

    nz = nocc // 2
    turned = [(t + TURN) % side for t in range(side)]

    def line(along, fixed, z, c):
        chips = [(t, fixed) if along == 0 else (fixed, t) for t in turned]
        return [(x * side + y) * nocc + 2 * z + c for x, y in chips]

    def summed(tiles, axes, groups):
        parts = lax.all_to_all(tiles, axes, 0, 0, tiled=True, axis_index_groups=groups)
        members = len(groups[0])
        parts = parts.reshape(members, tiles.shape[0] // members, *tiles.shape[1:])
        if parts.size < dense.size:
            return parts.astype(jnp.float32).sum(0).astype(jnp.bfloat16)
        return pl.pallas_call(
            add_parts,
            in_specs=[vmem],
            out_specs=vmem,
            out_shape=jax.ShapeDtypeStruct(parts.shape[1:], parts.dtype),
            compiler_params=pltpu.CompilerParams(vmem_limit_bytes=24 << 20),
            name="add_parts",
        )(parts)

    both = ("grp", "occ")
    lines = [line(c, fixed, z, c) for c in range(2) for z in range(nz) for fixed in range(side)]
    mine = summed(dense, both, lines)
    planes = []
    for c in range(2):
        for z in range(0, nz, 2):
            for fixed in range(side):
                even = line(1 - c, fixed, z, c)
                odd = line(1 - c, fixed, (z + 1 - 2 * c) % nz, c)
                planes.append(even + odd)
    mine = summed(mine, both, planes)
    order = [(z + START) % (nz // 2) for z in range(nz // 2)]
    columns = [[2 * (2 * z + e) + c for z in order] for e in range(2) for c in range(2)]
    blocks = mine.reshape(each, nz // 2, LANES, tile).transpose(1, 0, 2, 3)
    blocks = blocks.reshape(nz // 2 * each, LANES, tile)
    return summed(blocks, "occ", columns).transpose(1, 0, 2)


def solution(mesh):
    return jax.shard_map(
        functools.partial(local, mesh.shape["grp"], mesh.shape["occ"]),
        mesh=mesh,
        in_specs=(
            P(("grp", "occ"), None, None),
            P(("grp", "occ"), None, None),
            P(("grp", "occ"), None),
            P("grp", None),
            P("grp"),
            P(),
        ),
        out_specs=P("occ", "grp", None),
        check_vma=False,
    )
```

```python
import functools
import math

import jax
import jax.numpy as jnp
from jax import lax
from jax.experimental import pallas as pl
from jax.experimental.pallas import tpu as pltpu
from jax.sharding import PartitionSpec as P

LANES = 8
TURN = 2
START = 5


def amplitudes(kdom, tile, me_ref, cnt_hbm, b_hbm, q_hbm, inv_hbm, keep_ref, send_hbm, cnt, b_buf, q_buf, inv, scaled, send_ref, small, sems):
    own = b_buf.shape[0]
    me = me_ref[0]
    counts = pltpu.make_async_copy(cnt_hbm, cnt, small.at[0])
    counts.start()
    gaps = pltpu.make_async_copy(inv_hbm, inv, small.at[1])
    gaps.start()

    def fetch(i):
        return (
            pltpu.make_async_copy(q_hbm.at[i], q_buf.at[i], sems.at[0, i]),
            pltpu.make_async_copy(b_hbm.at[i], b_buf.at[i], sems.at[1, i]),
        )

    def store(i):
        tiles = pl.ds(i * kdom, kdom)
        return pltpu.make_async_copy(send_ref.at[tiles], send_hbm.at[tiles], sems.at[2, i])

    for i in range(own):
        for copy in fetch(i):
            copy.start()
    counts.wait()
    gaps.wait()
    first = me % 2 == 0

    def contract(i):
        for copy in fetch(i):
            copy.wait()
        q = q_buf[i]
        at = lax.broadcasted_iota(jnp.int32, q.shape, 0)
        used = cnt[me * own + i] * tile
        q = jnp.where(at < used, q.astype(jnp.float32), 0.0).astype(jnp.bfloat16)
        h = lax.dot_general(b_buf[i], q, (((0,), (0,)), ((), ())), preferred_element_type=jnp.float32)
        h = h * inv[pl.ds(i, 1), :]
        nb, nosv = h.shape
        h = h.reshape(nb // (4 * LANES), 4, LANES, nosv)
        h = jnp.concatenate([h[START:], h[:START]], 0)
        even = jnp.concatenate([h[:, z].reshape(nb // 4, nosv) for z in (0, 2)], 0)
        odd = jnp.concatenate([h[:, z].reshape(nb // 4, nosv) for z in (1, 3)], 0)
        scaled[i] = jnp.concatenate([jnp.where(first, even, odd), jnp.where(first, odd, even)], 0).astype(scaled.dtype)

    def expand(i):
        half = scaled.shape[1] // 2
        y = lax.dot_general(scaled[i], q_buf[i], (((1,), (1,)), ((), ())), preferred_element_type=jnp.float32)
        y = y.astype(jnp.bfloat16)
        for k in range(kdom):
            keep_ref[i * kdom + k] = y[:half, k * tile : (k + 1) * tile]
            send_ref[i * kdom + k] = y[half:, k * tile : (k + 1) * tile]
        store(i).start()

    pl.loop(0, own, unroll=own)(contract)
    pl.loop(0, own, unroll=own)(expand)

    @pl.loop(0, own)
    def _(i):
        store(i).wait()


def place(each, heads, after, tiles_ref, out_ref, base):
    count = tiles_ref.shape[0]
    rows = out_ref.shape[1]

    @pl.loop(0, count)
    def _(t):
        slot = heads[t]

        @pl.when(slot >= 0)
        def _():
            at = slot // each * (2 * each) + slot % each
            following = after[t]

            def put(total):
                out_ref[at] = total[:rows]
                out_ref[at + each] = total[rows:]

            def summed(total):
                def body(state):
                    n, total = state
                    return after[n], total + tiles_ref[n].astype(jnp.float32)

                total = total + tiles_ref[t].astype(jnp.float32)
                put(lax.while_loop(lambda state: state[0] < count, body, (following, total))[1].astype(out_ref.dtype))

            if base is None:
                pl.when(following >= count)(lambda: put(tiles_ref[t]))
                pl.when(following < count)(lambda: summed(0.0))
            else:
                summed(jnp.concatenate([base[at], base[at + each]], 0).astype(jnp.float32))


def place_own(each, heads, after, own_ref, out_ref):
    out_ref[...] = jnp.zeros_like(out_ref)
    place(each, heads, after, own_ref, out_ref, None)


def place_got(each, heads, after, got_ref, base_ref, out_ref):
    place(each, heads, after, got_ref, out_ref, out_ref)


def add_parts(parts_ref, out_ref):
    @pl.loop(0, out_ref.shape[0])
    def _(t):
        total = parts_ref[0, t].astype(jnp.float32)
        for part in range(1, parts_ref.shape[0]):
            total = total + parts_ref[part, t].astype(jnp.float32)
        out_ref[t] = total.astype(out_ref.dtype)


def local(ngrp, nocc, b_ints, osv_vecs, inv_denom, domains, dom_count, owner_slot):
    own, rows, nb = b_ints.shape
    kdom = domains.shape[1]
    tile = rows // kdom
    nosv = osv_vecs.shape[2]
    ntiles = owner_slot.shape[0]
    me = lax.axis_index("occ")
    core = me % 2
    half = nb // 2
    vmem = pl.BlockSpec(memory_space=pltpu.VMEM)
    smem = pl.BlockSpec(memory_space=pltpu.SMEM)
    hbm = pl.BlockSpec(memory_space=pl.ANY)

    half_tiles = jax.ShapeDtypeStruct((own * kdom, half, tile), jnp.bfloat16)
    kept, sent = pl.pallas_call(
        functools.partial(amplitudes, kdom, tile),
        in_specs=[smem, hbm, hbm, hbm, hbm],
        out_specs=[vmem, hbm],
        out_shape=[half_tiles, half_tiles],
        scratch_shapes=[
            pltpu.SMEM(dom_count.shape, jnp.int32),
            pltpu.VMEM(b_ints.shape, b_ints.dtype),
            pltpu.VMEM(osv_vecs.shape, osv_vecs.dtype),
            pltpu.VMEM(inv_denom.shape, inv_denom.dtype),
            pltpu.VMEM((own, nb, nosv), jnp.bfloat16),
            pltpu.VMEM(half_tiles.shape, half_tiles.dtype),
            pltpu.SemaphoreType.DMA((2,)),
            pltpu.SemaphoreType.DMA((3, own)),
        ],
        compiler_params=pltpu.CompilerParams(vmem_limit_bytes=52 << 20),
        cost_estimate=pl.CostEstimate(flops=4 * own * rows * nb * nosv, bytes_accessed=8 << 20, transcendentals=0),
        name="amplitudes",
    )(me.reshape(1), dom_count, b_ints, osv_vecs, inv_denom)

    got = lax.ppermute(sent, "occ", [(i, i ^ 1) for i in range(nocc)])

    base = (me - core) * own
    pair = lax.dynamic_slice_in_dim(domains, base, 2 * own, 0)
    counts = lax.dynamic_slice_in_dim(dom_count, base, 2 * own, 0)
    keep = jnp.arange(kdom, dtype=jnp.int32)[None, :] < counts[:, None]
    side = math.isqrt(ngrp)
    each = ntiles // ngrp
    owner, within = owner_slot // each, owner_slot % each
    along_x, along_y = (owner // side - TURN) % side, (owner % side - TURN) % side
    first, second = jnp.where(core == 0, along_x, along_y), jnp.where(core == 0, along_y, along_x)
    places = (first * side + second) * each + within
    looked = jnp.sum(jnp.where(pair[:, :, None] == jnp.arange(ntiles, dtype=jnp.int32), places, 0), axis=-1)
    slots = jnp.where(keep, looked, -1)
    slots = jnp.where(core == 0, slots, jnp.roll(slots, own, axis=0)).reshape(2, own * kdom)
    order = jnp.arange(own * kdom, dtype=jnp.int32)
    same = slots[:, :, None] == slots[:, None, :]
    earlier = jnp.any(same & (order[None, :] < order[:, None]), axis=2)
    heads = jnp.where(earlier, -1, slots)
    after = jnp.min(jnp.where(same & (order[None, :] > order[:, None]), order[None, :], own * kdom), axis=2)

    grid = jax.ShapeDtypeStruct((2 * ntiles, half // 2, tile), jnp.bfloat16)
    dense = pl.pallas_call(
        functools.partial(place_own, side * each),
        in_specs=[smem, smem, vmem],
        out_specs=vmem,
        out_shape=grid,
        compiler_params=pltpu.CompilerParams(vmem_limit_bytes=24 << 20),
        cost_estimate=pl.CostEstimate(flops=1 << 21, bytes_accessed=2 << 20, transcendentals=0),
        name="place_own",
    )(heads[0], after[0], kept)
    dense = pl.pallas_call(
        functools.partial(place_got, side * each),
        in_specs=[smem, smem, vmem, vmem],
        out_specs=vmem,
        out_shape=grid,
        input_output_aliases={3: 0},
        compiler_params=pltpu.CompilerParams(vmem_limit_bytes=24 << 20),
        name="place_got",
    )(heads[1], after[1], got, dense)

    nz = nocc // 2
    turned = [(t + TURN) % side for t in range(side)]

    def line(along, fixed, z, c):
        chips = [(t, fixed) if along == 0 else (fixed, t) for t in turned]
        return [(x * side + y) * nocc + 2 * z + c for x, y in chips]

    def summed(tiles, axes, groups):
        parts = lax.all_to_all(tiles, axes, 0, 0, tiled=True, axis_index_groups=groups)
        members = len(groups[0])
        parts = parts.reshape(members, tiles.shape[0] // members, *tiles.shape[1:])
        if parts.size < dense.size:
            return parts.astype(jnp.float32).sum(0).astype(jnp.bfloat16)
        return pl.pallas_call(
            add_parts,
            in_specs=[vmem],
            out_specs=vmem,
            out_shape=jax.ShapeDtypeStruct(parts.shape[1:], parts.dtype),
            compiler_params=pltpu.CompilerParams(vmem_limit_bytes=24 << 20),
            name="add_parts",
        )(parts)

    both = ("grp", "occ")
    lines = [line(c, fixed, z, c) for c in range(2) for z in range(nz) for fixed in range(side)]
    mine = summed(dense, both, lines)
    planes = []
    for c in range(2):
        for z in range(0, nz, 2):
            for fixed in range(side):
                even = line(1 - c, fixed, z, c)
                odd = line(1 - c, fixed, (z + 1 - 2 * c) % nz, c)
                planes.append(even + odd)
    mine = summed(mine, both, planes)
    order = [(z + START) % (nz // 2) for z in range(nz // 2)]
    columns = [[2 * (2 * z + e) + c for z in order] for e in range(2) for c in range(2)]
    blocks = mine.reshape(each, nz // 2, LANES, tile).transpose(1, 0, 2, 3)
    blocks = blocks.reshape(nz // 2 * each, LANES, tile)
    return summed(blocks, "occ", columns).transpose(1, 0, 2)


def solution(mesh):
    return jax.shard_map(
        functools.partial(local, mesh.shape["grp"], mesh.shape["occ"]),
        mesh=mesh,
        in_specs=(
            P(("grp", "occ"), None, None),
            P(("grp", "occ"), None, None),
            P(("grp", "occ"), None),
            P("grp", None),
            P("grp"),
            P(),
        ),
        out_specs=P("occ", "grp", None),
        check_vma=False,
    )
```

```python
import functools
import math

import jax
import jax.numpy as jnp
from jax import lax
from jax.experimental import pallas as pl
from jax.experimental.pallas import tpu as pltpu
from jax.sharding import PartitionSpec as P

LANES = 8
TURN = 2
START = 5


def amplitudes(kdom, tile, me_ref, cnt_hbm, b_hbm, q_hbm, inv_hbm, keep_ref, send_hbm, cnt, b_buf, q_buf, inv, scaled, send_ref, small, sems):
    own = b_buf.shape[0]
    me = me_ref[0]
    counts = pltpu.make_async_copy(cnt_hbm, cnt, small.at[0])
    counts.start()
    gaps = pltpu.make_async_copy(inv_hbm, inv, small.at[1])
    gaps.start()

    def fetch(i):
        return (
            pltpu.make_async_copy(q_hbm.at[i], q_buf.at[i], sems.at[0, i]),
            pltpu.make_async_copy(b_hbm.at[i], b_buf.at[i], sems.at[1, i]),
        )

    def store(i):
        tiles = pl.ds(i * kdom, kdom)
        return pltpu.make_async_copy(send_ref.at[tiles], send_hbm.at[tiles], sems.at[2, i])

    for i in range(own):
        for copy in fetch(i):
            copy.start()
    counts.wait()
    gaps.wait()
    first = me % 2 == 0

    def contract(i):
        for copy in fetch(i):
            copy.wait()
        q = q_buf[i]
        at = lax.broadcasted_iota(jnp.int32, q.shape, 0)
        used = cnt[me * own + i] * tile
        q = jnp.where(at < used, q.astype(jnp.float32), 0.0).astype(jnp.bfloat16)
        h = lax.dot_general(b_buf[i], q, (((0,), (0,)), ((), ())), preferred_element_type=jnp.float32)
        h = h * inv[pl.ds(i, 1), :]
        nb, nosv = h.shape
        h = h.reshape(nb // (4 * LANES), 4, LANES, nosv)
        h = jnp.concatenate([h[START:], h[:START]], 0)
        even = jnp.concatenate([h[:, z].reshape(nb // 4, nosv) for z in (2, 0)], 0)
        odd = jnp.concatenate([h[:, z].reshape(nb // 4, nosv) for z in (3, 1)], 0)
        scaled[i] = jnp.concatenate([jnp.where(first, even, odd), jnp.where(first, odd, even)], 0).astype(scaled.dtype)

    def expand(i):
        half = scaled.shape[1] // 2
        y = lax.dot_general(scaled[i], q_buf[i], (((1,), (1,)), ((), ())), preferred_element_type=jnp.float32)
        y = y.astype(jnp.bfloat16)
        for k in range(kdom):
            keep_ref[i * kdom + k] = y[:half, k * tile : (k + 1) * tile]
            send_ref[i * kdom + k] = y[half:, k * tile : (k + 1) * tile]
        store(i).start()

    pl.loop(0, own, unroll=own)(contract)
    pl.loop(0, own, unroll=own)(expand)

    @pl.loop(0, own)
    def _(i):
        store(i).wait()


def place(each, heads, after, tiles_ref, out_ref, base):
    count = tiles_ref.shape[0]
    rows = out_ref.shape[1]

    @pl.loop(0, count)
    def _(t):
        slot = heads[t]

        @pl.when(slot >= 0)
        def _():
            at = slot // each * (2 * each) + slot % each
            following = after[t]

            def put(total):
                out_ref[at] = total[:rows]
                out_ref[at + each] = total[rows:]

            def summed(total):
                def body(state):
                    n, total = state
                    return after[n], total + tiles_ref[n].astype(jnp.float32)

                total = total + tiles_ref[t].astype(jnp.float32)
                put(lax.while_loop(lambda state: state[0] < count, body, (following, total))[1].astype(out_ref.dtype))

            if base is None:
                pl.when(following >= count)(lambda: put(tiles_ref[t]))
                pl.when(following < count)(lambda: summed(0.0))
            else:
                summed(jnp.concatenate([base[at], base[at + each]], 0).astype(jnp.float32))


def place_own(each, heads, after, own_ref, out_ref):
    out_ref[...] = jnp.zeros_like(out_ref)
    place(each, heads, after, own_ref, out_ref, None)


def place_got(each, heads, after, got_ref, base_ref, out_ref):
    place(each, heads, after, got_ref, out_ref, out_ref)


def add_parts(parts_ref, out_ref):
    @pl.loop(0, out_ref.shape[0])
    def _(t):
        total = parts_ref[0, t].astype(jnp.float32)
        for part in range(1, parts_ref.shape[0]):
            total = total + parts_ref[part, t].astype(jnp.float32)
        out_ref[t] = total.astype(out_ref.dtype)


def local(ngrp, nocc, b_ints, osv_vecs, inv_denom, domains, dom_count, owner_slot):
    own, rows, nb = b_ints.shape
    kdom = domains.shape[1]
    tile = rows // kdom
    nosv = osv_vecs.shape[2]
    ntiles = owner_slot.shape[0]
    me = lax.axis_index("occ")
    core = me % 2
    half = nb // 2
    vmem = pl.BlockSpec(memory_space=pltpu.VMEM)
    smem = pl.BlockSpec(memory_space=pltpu.SMEM)
    hbm = pl.BlockSpec(memory_space=pl.ANY)

    half_tiles = jax.ShapeDtypeStruct((own * kdom, half, tile), jnp.bfloat16)
    kept, sent = pl.pallas_call(
        functools.partial(amplitudes, kdom, tile),
        in_specs=[smem, hbm, hbm, hbm, hbm],
        out_specs=[vmem, hbm],
        out_shape=[half_tiles, half_tiles],
        scratch_shapes=[
            pltpu.SMEM(dom_count.shape, jnp.int32),
            pltpu.VMEM(b_ints.shape, b_ints.dtype),
            pltpu.VMEM(osv_vecs.shape, osv_vecs.dtype),
            pltpu.VMEM(inv_denom.shape, inv_denom.dtype),
            pltpu.VMEM((own, nb, nosv), jnp.bfloat16),
            pltpu.VMEM(half_tiles.shape, half_tiles.dtype),
            pltpu.SemaphoreType.DMA((2,)),
            pltpu.SemaphoreType.DMA((3, own)),
        ],
        compiler_params=pltpu.CompilerParams(vmem_limit_bytes=52 << 20),
        cost_estimate=pl.CostEstimate(flops=4 * own * rows * nb * nosv, bytes_accessed=8 << 20, transcendentals=0),
        name="amplitudes",
    )(me.reshape(1), dom_count, b_ints, osv_vecs, inv_denom)

    got = lax.ppermute(sent, "occ", [(i, i ^ 1) for i in range(nocc)])

    base = (me - core) * own
    pair = lax.dynamic_slice_in_dim(domains, base, 2 * own, 0)
    counts = lax.dynamic_slice_in_dim(dom_count, base, 2 * own, 0)
    keep = jnp.arange(kdom, dtype=jnp.int32)[None, :] < counts[:, None]
    side = math.isqrt(ngrp)
    each = ntiles // ngrp
    owner, within = owner_slot // each, owner_slot % each
    along_x, along_y = (owner // side - TURN) % side, (owner % side - TURN) % side
    first, second = jnp.where(core == 0, along_x, along_y), jnp.where(core == 0, along_y, along_x)
    places = (first * side + second) * each + within
    looked = jnp.sum(jnp.where(pair[:, :, None] == jnp.arange(ntiles, dtype=jnp.int32), places, 0), axis=-1)
    slots = jnp.where(keep, looked, -1)
    slots = jnp.where(core == 0, slots, jnp.roll(slots, own, axis=0)).reshape(2, own * kdom)
    order = jnp.arange(own * kdom, dtype=jnp.int32)
    same = slots[:, :, None] == slots[:, None, :]
    earlier = jnp.any(same & (order[None, :] < order[:, None]), axis=2)
    heads = jnp.where(earlier, -1, slots)
    after = jnp.min(jnp.where(same & (order[None, :] > order[:, None]), order[None, :], own * kdom), axis=2)

    grid = jax.ShapeDtypeStruct((2 * ntiles, half // 2, tile), jnp.bfloat16)
    dense = pl.pallas_call(
        functools.partial(place_own, side * each),
        in_specs=[smem, smem, vmem],
        out_specs=vmem,
        out_shape=grid,
        compiler_params=pltpu.CompilerParams(vmem_limit_bytes=24 << 20),
        cost_estimate=pl.CostEstimate(flops=1 << 21, bytes_accessed=2 << 20, transcendentals=0),
        name="place_own",
    )(heads[0], after[0], kept)
    dense = pl.pallas_call(
        functools.partial(place_got, side * each),
        in_specs=[smem, smem, vmem, vmem],
        out_specs=vmem,
        out_shape=grid,
        input_output_aliases={3: 0},
        compiler_params=pltpu.CompilerParams(vmem_limit_bytes=24 << 20),
        name="place_got",
    )(heads[1], after[1], got, dense)

    nz = nocc // 2
    turned = [(t + TURN) % side for t in range(side)]

    def line(along, fixed, z, c):
        chips = [(t, fixed) if along == 0 else (fixed, t) for t in turned]
        return [(x * side + y) * nocc + 2 * z + c for x, y in chips]

    def summed(tiles, axes, groups):
        parts = lax.all_to_all(tiles, axes, 0, 0, tiled=True, axis_index_groups=groups)
        members = len(groups[0])
        parts = parts.reshape(members, tiles.shape[0] // members, *tiles.shape[1:])
        if parts.size < dense.size:
            return parts.astype(jnp.float32).sum(0).astype(jnp.bfloat16)
        return pl.pallas_call(
            add_parts,
            in_specs=[vmem],
            out_specs=vmem,
            out_shape=jax.ShapeDtypeStruct(parts.shape[1:], parts.dtype),
            compiler_params=pltpu.CompilerParams(vmem_limit_bytes=24 << 20),
            name="add_parts",
        )(parts)

    both = ("grp", "occ")
    lines = [line(c, fixed, z, c) for c in range(2) for z in range(nz) for fixed in range(side)]
    mine = summed(dense, both, lines)
    planes = []
    for c in range(2):
        for z in range(0, nz, 2):
            for fixed in range(side):
                even = line(1 - c, fixed, z, c)
                odd = line(1 - c, fixed, (z + 1 - 2 * c) % nz, c)
                planes.append(odd + even)
    mine = summed(mine, both, planes)
    order = [(z + START) % (nz // 2) for z in range(nz // 2)]
    columns = [[2 * (2 * z + e) + c for z in order] for e in range(2) for c in range(2)]
    blocks = mine.reshape(each, nz // 2, LANES, tile).transpose(1, 0, 2, 3)
    blocks = blocks.reshape(nz // 2 * each, LANES, tile)
    return summed(blocks, "occ", columns).transpose(1, 0, 2)


def solution(mesh):
    return jax.shard_map(
        functools.partial(local, mesh.shape["grp"], mesh.shape["occ"]),
        mesh=mesh,
        in_specs=(
            P(("grp", "occ"), None, None),
            P(("grp", "occ"), None, None),
            P(("grp", "occ"), None),
            P("grp", None),
            P("grp"),
            P(),
        ),
        out_specs=P("occ", "grp", None),
        check_vma=False,
    )
```

```python
import functools
import math

import jax
import jax.numpy as jnp
from jax import lax
from jax.experimental import pallas as pl
from jax.experimental.pallas import tpu as pltpu
from jax.sharding import PartitionSpec as P

LANES = 8
TURN = 2
START = 4


def amplitudes(kdom, tile, me_ref, cnt_hbm, b_hbm, q_hbm, inv_hbm, keep_ref, send_hbm, cnt, b_buf, q_buf, inv, scaled, send_ref, small, sems):
    own = b_buf.shape[0]
    me = me_ref[0]
    counts = pltpu.make_async_copy(cnt_hbm, cnt, small.at[0])
    counts.start()
    gaps = pltpu.make_async_copy(inv_hbm, inv, small.at[1])
    gaps.start()

    def fetch(i):
        return (
            pltpu.make_async_copy(q_hbm.at[i], q_buf.at[i], sems.at[0, i]),
            pltpu.make_async_copy(b_hbm.at[i], b_buf.at[i], sems.at[1, i]),
        )

    def store(i):
        tiles = pl.ds(i * kdom, kdom)
        return pltpu.make_async_copy(send_ref.at[tiles], send_hbm.at[tiles], sems.at[2, i])

    for i in range(own):
        for copy in fetch(i):
            copy.start()
    counts.wait()
    gaps.wait()
    first = me % 2 == 0

    def contract(i):
        for copy in fetch(i):
            copy.wait()
        q = q_buf[i]
        at = lax.broadcasted_iota(jnp.int32, q.shape, 0)
        used = cnt[me * own + i] * tile
        q = jnp.where(at < used, q.astype(jnp.float32), 0.0).astype(jnp.bfloat16)
        h = lax.dot_general(b_buf[i], q, (((0,), (0,)), ((), ())), preferred_element_type=jnp.float32)
        h = h * inv[pl.ds(i, 1), :]
        nb, nosv = h.shape
        h = h.reshape(nb // (4 * LANES), 4, LANES, nosv)
        h = jnp.concatenate([h[START:], h[:START]], 0)
        even = jnp.concatenate([h[:, z].reshape(nb // 4, nosv) for z in (2, 0)], 0)
        odd = jnp.concatenate([h[:, z].reshape(nb // 4, nosv) for z in (3, 1)], 0)
        scaled[i] = jnp.concatenate([jnp.where(first, even, odd), jnp.where(first, odd, even)], 0).astype(scaled.dtype)

    def expand(i):
        half = scaled.shape[1] // 2
        y = lax.dot_general(scaled[i], q_buf[i], (((1,), (1,)), ((), ())), preferred_element_type=jnp.float32)
        y = y.astype(jnp.bfloat16)
        for k in range(kdom):
            keep_ref[i * kdom + k] = y[:half, k * tile : (k + 1) * tile]
            send_ref[i * kdom + k] = y[half:, k * tile : (k + 1) * tile]
        store(i).start()

    pl.loop(0, own, unroll=own)(contract)
    pl.loop(0, own, unroll=own)(expand)

    @pl.loop(0, own)
    def _(i):
        store(i).wait()


def place(each, heads, after, tiles_ref, out_ref, base):
    count = tiles_ref.shape[0]
    rows = out_ref.shape[1]

    @pl.loop(0, count)
    def _(t):
        slot = heads[t]

        @pl.when(slot >= 0)
        def _():
            at = slot // each * (2 * each) + slot % each
            following = after[t]

            def put(total):
                out_ref[at] = total[:rows]
                out_ref[at + each] = total[rows:]

            def summed(total):
                def body(state):
                    n, total = state
                    return after[n], total + tiles_ref[n].astype(jnp.float32)

                total = total + tiles_ref[t].astype(jnp.float32)
                put(lax.while_loop(lambda state: state[0] < count, body, (following, total))[1].astype(out_ref.dtype))

            if base is None:
                pl.when(following >= count)(lambda: put(tiles_ref[t]))
                pl.when(following < count)(lambda: summed(0.0))
            else:
                summed(jnp.concatenate([base[at], base[at + each]], 0).astype(jnp.float32))


def place_own(each, heads, after, own_ref, out_ref):
    out_ref[...] = jnp.zeros_like(out_ref)
    place(each, heads, after, own_ref, out_ref, None)


def place_got(each, heads, after, got_ref, base_ref, out_ref):
    place(each, heads, after, got_ref, out_ref, out_ref)


def add_parts(parts_ref, out_ref):
    @pl.loop(0, out_ref.shape[0])
    def _(t):
        total = parts_ref[0, t].astype(jnp.float32)
        for part in range(1, parts_ref.shape[0]):
            total = total + parts_ref[part, t].astype(jnp.float32)
        out_ref[t] = total.astype(out_ref.dtype)


def local(ngrp, nocc, b_ints, osv_vecs, inv_denom, domains, dom_count, owner_slot):
    own, rows, nb = b_ints.shape
    kdom = domains.shape[1]
    tile = rows // kdom
    nosv = osv_vecs.shape[2]
    ntiles = owner_slot.shape[0]
    me = lax.axis_index("occ")
    core = me % 2
    half = nb // 2
    vmem = pl.BlockSpec(memory_space=pltpu.VMEM)
    smem = pl.BlockSpec(memory_space=pltpu.SMEM)
    hbm = pl.BlockSpec(memory_space=pl.ANY)

    half_tiles = jax.ShapeDtypeStruct((own * kdom, half, tile), jnp.bfloat16)
    kept, sent = pl.pallas_call(
        functools.partial(amplitudes, kdom, tile),
        in_specs=[smem, hbm, hbm, hbm, hbm],
        out_specs=[vmem, hbm],
        out_shape=[half_tiles, half_tiles],
        scratch_shapes=[
            pltpu.SMEM(dom_count.shape, jnp.int32),
            pltpu.VMEM(b_ints.shape, b_ints.dtype),
            pltpu.VMEM(osv_vecs.shape, osv_vecs.dtype),
            pltpu.VMEM(inv_denom.shape, inv_denom.dtype),
            pltpu.VMEM((own, nb, nosv), jnp.bfloat16),
            pltpu.VMEM(half_tiles.shape, half_tiles.dtype),
            pltpu.SemaphoreType.DMA((2,)),
            pltpu.SemaphoreType.DMA((3, own)),
        ],
        compiler_params=pltpu.CompilerParams(vmem_limit_bytes=52 << 20),
        cost_estimate=pl.CostEstimate(flops=4 * own * rows * nb * nosv, bytes_accessed=8 << 20, transcendentals=0),
        name="amplitudes",
    )(me.reshape(1), dom_count, b_ints, osv_vecs, inv_denom)

    got = lax.ppermute(sent, "occ", [(i, i ^ 1) for i in range(nocc)])

    base = (me - core) * own
    pair = lax.dynamic_slice_in_dim(domains, base, 2 * own, 0)
    counts = lax.dynamic_slice_in_dim(dom_count, base, 2 * own, 0)
    keep = jnp.arange(kdom, dtype=jnp.int32)[None, :] < counts[:, None]
    side = math.isqrt(ngrp)
    each = ntiles // ngrp
    owner, within = owner_slot // each, owner_slot % each
    along_x, along_y = (owner // side - TURN) % side, (owner % side - TURN) % side
    first, second = jnp.where(core == 0, along_x, along_y), jnp.where(core == 0, along_y, along_x)
    places = (first * side + second) * each + within
    looked = jnp.sum(jnp.where(pair[:, :, None] == jnp.arange(ntiles, dtype=jnp.int32), places, 0), axis=-1)
    slots = jnp.where(keep, looked, -1)
    slots = jnp.where(core == 0, slots, jnp.roll(slots, own, axis=0)).reshape(2, own * kdom)
    order = jnp.arange(own * kdom, dtype=jnp.int32)
    same = slots[:, :, None] == slots[:, None, :]
    earlier = jnp.any(same & (order[None, :] < order[:, None]), axis=2)
    heads = jnp.where(earlier, -1, slots)
    after = jnp.min(jnp.where(same & (order[None, :] > order[:, None]), order[None, :], own * kdom), axis=2)

    grid = jax.ShapeDtypeStruct((2 * ntiles, half // 2, tile), jnp.bfloat16)
    dense = pl.pallas_call(
        functools.partial(place_own, side * each),
        in_specs=[smem, smem, vmem],
        out_specs=vmem,
        out_shape=grid,
        compiler_params=pltpu.CompilerParams(vmem_limit_bytes=24 << 20),
        cost_estimate=pl.CostEstimate(flops=1 << 21, bytes_accessed=2 << 20, transcendentals=0),
        name="place_own",
    )(heads[0], after[0], kept)
    dense = pl.pallas_call(
        functools.partial(place_got, side * each),
        in_specs=[smem, smem, vmem, vmem],
        out_specs=vmem,
        out_shape=grid,
        input_output_aliases={3: 0},
        compiler_params=pltpu.CompilerParams(vmem_limit_bytes=24 << 20),
        name="place_got",
    )(heads[1], after[1], got, dense)

    nz = nocc // 2
    turned = [(t + TURN) % side for t in range(side)]

    def line(along, fixed, z, c):
        chips = [(t, fixed) if along == 0 else (fixed, t) for t in turned]
        return [(x * side + y) * nocc + 2 * z + c for x, y in chips]

    def summed(tiles, axes, groups):
        parts = lax.all_to_all(tiles, axes, 0, 0, tiled=True, axis_index_groups=groups)
        members = len(groups[0])
        parts = parts.reshape(members, tiles.shape[0] // members, *tiles.shape[1:])
        if parts.size < dense.size:
            return parts.astype(jnp.float32).sum(0).astype(jnp.bfloat16)
        return pl.pallas_call(
            add_parts,
            in_specs=[vmem],
            out_specs=vmem,
            out_shape=jax.ShapeDtypeStruct(parts.shape[1:], parts.dtype),
            compiler_params=pltpu.CompilerParams(vmem_limit_bytes=24 << 20),
            name="add_parts",
        )(parts)

    both = ("grp", "occ")
    lines = [line(c, fixed, z, c) for c in range(2) for z in range(nz) for fixed in range(side)]
    mine = summed(dense, both, lines)
    planes = []
    for c in range(2):
        for z in range(0, nz, 2):
            for fixed in range(side):
                even = line(1 - c, fixed, z, c)
                odd = line(1 - c, fixed, (z + 1 - 2 * c) % nz, c)
                planes.append(odd + even)
    mine = summed(mine, both, planes)
    order = [(z + START) % (nz // 2) for z in range(nz // 2)]
    columns = [[2 * (2 * z + e) + c for z in order] for e in range(2) for c in range(2)]
    blocks = mine.reshape(each, nz // 2, LANES, tile).transpose(1, 0, 2, 3)
    blocks = blocks.reshape(nz // 2 * each, LANES, tile)
    return summed(blocks, "occ", columns).transpose(1, 0, 2)


def solution(mesh):
    return jax.shard_map(
        functools.partial(local, mesh.shape["grp"], mesh.shape["occ"]),
        mesh=mesh,
        in_specs=(
            P(("grp", "occ"), None, None),
            P(("grp", "occ"), None, None),
            P(("grp", "occ"), None),
            P("grp", None),
            P("grp"),
            P(),
        ),
        out_specs=P("occ", "grp", None),
        check_vma=False,
    )
```
